1024 devices in a mesh: wide: 128 (over y, z), narrow: 8 (over x, core).
Axes of the slice: x: 4, y: 8, z: 16, core: 2. Of those that a mesh axis runs over, the one named last changes fastest.
Arguments:
- fine_blocks: bfloat16 [2048, 5, 192, 192], P(('wide', 'narrow')), may hold values from -6 to 6
- prolong_blocks: bfloat16 [2048, 2, 192, 192], P(('wide', 'narrow')), may hold values from -0.4375 to 0.4375
- agg_start: int32 [2048, 2], P(('wide', 'narrow')), may hold values from 0 to 255, as said below
Outputs:
- coarse_blocks: bfloat16 [2048, 17, 192, 192], P(('wide', 'narrow'))
- coarse_numbers: int32 [2048], P(('wide', 'narrow'))
The draws below stay inside these ranges and needn't reach their ends.
Inputs may be any that keep to these rules, and one draw needn't show every extreme that they name: Along every line of constant second coordinate, aggregates are runs of one or two consecutive pencils, the first pencil of a line always begins one, and the last pencil of the line of second coordinate 0 always begins one. agg_start[i, 0] is the first coordinate of the first pencil of the aggregate holding pencil i; agg_start[i, 1] is that of the aggregate holding the pencil just before i on its line, and equals agg_start[i, 0] at the line's first pencil.
All inputs are finite; a program needn't handle non-finite values.
Results may differ from the reference program's by a relative error of at most 0.0011.
The reference program's roundings to bfloat16 on the way (of `products`) count: a program that leaves them out, or rounds other values in their place, can miss the bound.
Values may be sent and summed in bfloat16 or wider, within the bound.
A program may use at most 128 MiB of HBM per device.

```python
import jax
import jax.numpy as jnp
from jax import lax

FB = 192
CB = 192
ROWS = 2
NEIGH = 5
SLOTS = 17
NX = 256
NY = 8
NBLK = 2048
N_WIDE = 128
N_NARROW = 8


def draw_agg_start(key, part):
    key = jax.random.fold_in(key, 11)
    coins = jax.random.randint(key, (NX, NY), 0, 2, dtype=jnp.int32)
    line_ids = jnp.arange(NY, dtype=jnp.int32)

    def advance(previous, inputs):
        position, coin = inputs
        forced = (position == 0) | (position == NX - 1) & (line_ids == 0)
        flag = jnp.where(forced, 1, jnp.maximum(coin, 1 - previous)).astype(jnp.int32)
        return (flag, flag)
    unused, flags = lax.scan(advance, jnp.ones((NY,), jnp.int32), (jnp.arange(NX, dtype=jnp.int32), coins))
    xgrid = jnp.arange(NX, dtype=jnp.int32)[:, None]
    first = xgrid - (1 - flags)
    before = jnp.concatenate([first[:1], first[:-1]], axis=0)
    paired = jnp.stack([first, before], axis=-1)
    return paired.reshape(N_WIDE, ROWS, NY, 2).transpose(0, 2, 1, 3).reshape(NX * NY, 2).astype(jnp.int32)


def level_of(key, shape, split, low, high):
    def one(axis_at, blocks):
        steps = jax.random.uniform(jax.random.fold_in(jax.random.fold_in(key, 6), axis_at), (blocks,), jnp.float32, low / len(split), high / len(split))
        return jnp.repeat(jnp.exp(steps), shape[axis_at] // blocks).reshape((-1,) + (1,) * (len(shape) - axis_at - 1))

    gain = one(*split[0])
    for cut in split[1:]:
        gain = gain * one(*cut)
    return gain


def centred(rng, shape, width, limit, split=(), kind=jnp.bfloat16):
    values = jax.random.normal(rng, shape, jnp.float32) * width
    if len(split) > 0:
        values = level_of(rng, shape, split, -0.22, 0.18) * values
    return jnp.clip(values, min=-limit, max=limit).astype(kind)


def setup_inputs(seed: int = 0) -> dict:
    keys = jax.random.split(jax.random.key(seed), 4)
    fine_blocks = centred(keys[0], (NBLK, NEIGH, FB, FB), 1.0, 6.0, ((0, 1024),))
    prolong_blocks = centred(keys[1], (NBLK, 2, FB, CB), FB ** -0.5, 0.4375, ((0, 1024),))
    agg_start = draw_agg_start(jax.random.fold_in(keys[3], 71), 0)
    return {"fine_blocks": fine_blocks, "prolong_blocks": prolong_blocks, "agg_start": agg_start}


slot_offsets = (3, 3, 3, 9, 14)


def to_grid(array):
    lead = array.shape[1:]
    return array.reshape((N_WIDE, N_NARROW, ROWS) + lead).swapaxes(1, 2).reshape((NX, NY) + lead)


def from_grid(grid):
    lead = grid.shape[2:]
    return grid.reshape((N_WIDE, ROWS, NY) + lead).swapaxes(1, 2).reshape((NBLK,) + lead)


def reference(fine_blocks, prolong_blocks, agg_start):
    agrid = to_grid(fine_blocks)
    pgrid = to_grid(prolong_blocks)
    sgrid = to_grid(agg_start)
    ppad = jnp.pad(pgrid, ((1, 1), (1, 1), (0, 0), (0, 0), (0, 0)))
    spad = jnp.pad(sgrid, ((1, 1), (1, 1), (0, 0)))

    def line_products(xpos):
        lines = lax.dynamic_slice_in_dim(ppad, xpos, 3, 0)
        nearby = jnp.stack([lines[1, 1:-1], lines[0, 1:-1], lines[2, 1:-1], lines[1, :-2], lines[1, 2:]], axis=1)
        blocks = lax.dynamic_index_in_dim(agrid, xpos, 0, keepdims=False)
        return jnp.einsum('ykfg,ykqgc->ykqfc', blocks.astype(jnp.float32), nearby.astype(jnp.float32)).astype(jnp.bfloat16)

    products = lax.map(line_products, jnp.arange(NX, dtype=jnp.int32))
    near_start = jnp.stack([spad[1:-1, 1:-1], spad[:-2, 1:-1], spad[2:, 1:-1], spad[1:-1, :-2], spad[1:-1, 2:]], axis=2)
    prod_ext = jnp.pad(products, ((0, 2), (0, 0), (0, 0), (0, 0), (0, 0), (0, 0)))
    prol_ext = jnp.pad(pgrid, ((0, 2), (0, 0), (0, 0), (0, 0), (0, 0)))
    start_ext = jnp.pad(sgrid, ((0, 2), (0, 0), (0, 0)), constant_values=-1)
    near_ext = jnp.pad(near_start, ((0, 2), (0, 0), (0, 0), (0, 0)))
    offsets = jnp.array(slot_offsets, jnp.int32)
    slot_range = jnp.arange(SLOTS, dtype=jnp.int32)

    def coarse_row(xpos):
        summed = jnp.zeros((NY, SLOTS, CB, CB), jnp.float32)
        for ahead, column in ((0, 0), (0, 1), (1, 0), (1, 1), (2, 1)):
            pencil = xpos + ahead
            starts_here = lax.dynamic_index_in_dim(start_ext, pencil, 0, keepdims=False)[:, column]
            matched = starts_here == xpos
            prolong = lax.dynamic_index_in_dim(prol_ext, pencil, 0, keepdims=False)[:, column]
            blocks = lax.dynamic_index_in_dim(prod_ext, pencil, 0, keepdims=False)
            nears = lax.dynamic_index_in_dim(near_ext, pencil, 0, keepdims=False)
            terms = jnp.einsum('yfc,ykqfd->ykqcd', prolong.astype(jnp.float32), blocks.astype(jnp.float32))
            column_slot = offsets[None, :, None] + nears - xpos
            onehot = ((column_slot[..., None] == slot_range) & matched[:, None, None, None]).astype(jnp.float32)
            summed = summed + jnp.einsum('ykqt,ykqcd->ytcd', onehot, terms, precision=lax.Precision.HIGHEST)
        return summed.astype(jnp.bfloat16)

    coarse_grid = lax.map(coarse_row, jnp.arange(NX, dtype=jnp.int32))
    coarse_blocks = from_grid(coarse_grid)
    pencil_index = jnp.arange(NBLK, dtype=jnp.int32)
    xcoord = (pencil_index // (ROWS * NY)) * ROWS + pencil_index % ROWS
    flags = (agg_start[:, 0] == xcoord).astype(jnp.int32)
    coarse_numbers = jnp.where(flags == 1, jnp.cumsum(flags).astype(jnp.int32) - 1, -1).astype(jnp.int32)
    return (coarse_blocks, coarse_numbers)
```

```python
import functools

import jax
import jax.numpy as jnp
from jax import lax
from jax.experimental import pallas as pl
from jax.experimental.pallas import tpu as pltpu
from jax.sharding import PartitionSpec as P

SLOTS = 17
ZDIM = 16
YDIM = 8
NDIM = 8
WDIM = 128
B = 192
W2 = 384
MESH = pl.DeviceIdType.MESH
BF = jnp.bfloat16
F32 = jnp.float32
COUNT_LANE = 4


def pack(x, y):
    lane = lax.broadcasted_iota(jnp.int32, (B, 128), 1)
    xh = jnp.concatenate([x[:, 128:].astype(F32), jnp.zeros((B, 64), F32)], axis=1)
    yh = jnp.concatenate([jnp.zeros((B, 64), F32), y[:, 128:].astype(F32)], axis=1)
    mid = jnp.where(lane < 64, xh, yh).astype(BF)
    return jnp.concatenate([x[:, :128], mid, y[:, :128]], axis=1)


def rows_first(pp):
    return jnp.concatenate([pp, jnp.zeros((64, W2), BF)], axis=0)


def rows_second(pp):
    return jnp.concatenate([jnp.zeros((64, W2), BF), pp[128:], pp[:128]], axis=0)


def mul(a, b):
    return jnp.dot(a, b, preferred_element_type=F32).astype(BF)


def exchange_kernel(
    a_hbm, p_hbm, start_ref,
    prods, pt, ints,
    a_raw, p_raw, pp, pp_up, pp_dn, pp_s, pp_su,
    a_send, a_recv, one_recv, prod_recv,
    own_tile, g1, tile2, r_up2, c_in, c_out, t_in, o_in, g3, o_out,
    local_sem, ssem, rsem, gs, gr, ys, yr, up_ready, low_ready,
):
    w = lax.axis_index("wide")
    n = lax.axis_index("narrow")
    y = w // ZDIM
    z = w % ZDIM
    has_low = w > 0
    has_up = w < WDIM - 1
    low_w = jnp.maximum(w - 1, 0)
    up_w = jnp.minimum(w + 1, WDIM - 1)
    first = z == 0
    last = z == ZDIM - 1
    has_left = n > 0
    has_right = n < NDIM - 1
    left = jnp.maximum(n - 1, 0)
    right = jnp.minimum(n + 1, NDIM - 1)

    load_p = pltpu.make_async_copy(p_hbm, p_raw, local_sem.at[0])
    load_a = pltpu.make_async_copy(a_hbm, a_raw, local_sem.at[1])
    load_p.start()
    load_a.start()

    barrier = pltpu.get_barrier_semaphore()

    def greet(dev):
        pl.semaphore_signal(barrier, inc=1, device_id=dev, device_id_type=MESH)

    @pl.when(z < ZDIM - 1)
    def _():
        greet((up_w, n))

    for d in range(1, NDIM):
        greet((w, lax.rem(n + d, NDIM)))

    @pl.when(first)
    def _():
        for d in range(1, YDIM):
            greet((lax.rem(y + d, YDIM) * ZDIM, n))
        greet((w + ZDIM - 1, n))

    @pl.when(first & has_low)
    def _():
        greet((low_w, n))

    lane = lax.broadcasted_iota(jnp.int32, (8, 128), 1)
    sub = lax.broadcasted_iota(jnp.int32, (8, 128), 0)
    s00, s01, s10, s11 = (start_ref[i, j] for i in range(2) for j in range(2))
    count = (s00 == 2 * w).astype(jnp.int32) + (s10 == 2 * w + 1).astype(jnp.int32)
    tile = jnp.zeros((8, 128), jnp.int32)
    for at, value in enumerate((s00, s01, s10, s11, count)):
        tile = jnp.where(lane == at, value, tile)
    own_tile[...] = tile

    load_p.wait()
    for r in range(2):
        pp[r] = pack(p_raw[r, 0], p_raw[r, 1])

    heard = (
        NDIM - 1
        + jnp.where(first, YDIM - 1, 1)
        + jnp.where(last, 1, 0)
        + jnp.where(last & has_up, 1, 0)
    )
    pl.semaphore_wait(barrier, heard)

    @pl.when(z > 0)
    def _():
        pl.semaphore_signal(up_ready, inc=1, device_id=(low_w, n), device_id_type=MESH)

    @pl.when(last & has_up)
    def _():
        pl.semaphore_signal(low_ready, inc=1, device_id=(up_w, n), device_id_type=MESH)

    def remote(src, dst, at, dev):
        return pltpu.make_async_remote_copy(
            src_ref=src, dst_ref=dst, send_sem=ssem.at[at], recv_sem=rsem.at[at],
            device_id=dev, device_id_type=MESH)

    low, up = (low_w, n), (up_w, n)
    pp_low = remote(pp, pp_up, 0, low)
    pp_high = remote(pp.at[1], pp_dn, 1, up)
    pp_left = remote(pp, pp_s.at[1], 2, (w, left))
    pp_right = remote(pp, pp_s.at[0], 3, (w, right))
    rel_left = remote(pp_up, pp_su.at[1], 4, (w, left))
    rel_right = remote(pp_up, pp_su.at[0], 5, (w, right))
    a_low = [remote(a_send.at[q], a_recv.at[q], 6 + q, low) for q in range(4)]
    one_low = remote(a_raw.at[1, 1], one_recv, 10, low)
    prod_low = remote(prods.at[1, 2], prod_recv, 11, low)
    tile_low = remote(tile2, ints.at[pl.ds(16, 8)], 12, low)
    tile_high = remote(tile2, ints.at[pl.ds(0, 8)], 13, up)
    tile_rel = remote(ints.at[pl.ds(16, 8)], ints.at[pl.ds(24, 8)], 14, low)
    chain_up = remote(c_out, c_in, 15, up)
    chain_wrap = remote(c_out, t_in, 16, (y * ZDIM, n))
    chain_two = remote(o_out, o_in, 17, up)
    gathers = []
    for d in range(1, NDIM):
        gathers.append(pltpu.make_async_remote_copy(
            src_ref=own_tile, dst_ref=g1.at[d], send_sem=gs.at[d], recv_sem=gr.at[d],
            device_id=(w, lax.rem(n + d, NDIM)), device_id_type=MESH))
    totals = []
    for d in range(1, YDIM):
        totals.append(pltpu.make_async_remote_copy(
            src_ref=t_in, dst_ref=g3.at[d], send_sem=ys.at[d], recv_sem=yr.at[d],
            device_id=(lax.rem(y + d, YDIM) * ZDIM, n), device_id_type=MESH))

    for c in gathers:
        c.start()
    pl.when(has_low & ~first)(pp_low.start)
    pl.when(has_left)(pp_left.start)
    pl.when(has_right)(pp_right.start)

    load_a.wait()
    for q, ((i0, k0), (i1, k1)) in enumerate(
        (((0, 0), (0, 1)), ((0, 2), (1, 0)), ((0, 3), (0, 4)), ((1, 3), (1, 4)))):
        a_send[q] = pack(a_raw[i0, k0], a_raw[i1, k1])
        pl.when(has_low & ~first)(a_low[q].start)
    pl.when(has_low & ~first)(one_low.start)

    @pl.when(jnp.logical_not(has_up))
    def _():
        pp_up[...] = jnp.zeros_like(pp_up)
        a_recv[...] = jnp.zeros_like(a_recv)
        one_recv[...] = jnp.zeros_like(one_recv)
        prod_recv[...] = jnp.zeros_like(prod_recv)
        ints[16:32] = jnp.zeros((16, 128), jnp.int32)

    @pl.when(jnp.logical_not(has_low))
    def _():
        pp_dn[...] = jnp.zeros_like(pp_dn)
        ints[0:8] = jnp.zeros((8, 128), jnp.int32)

    for side, there in ((0, has_left), (1, has_right)):
        @pl.when(jnp.logical_not(there))
        def _():
            pp_s[side] = jnp.zeros((2, B, W2), BF)
            pp_su[side] = jnp.zeros((2, B, W2), BF)

    for c in gathers:
        c.wait_recv()
    g1[0] = own_tile[...]
    before = jnp.zeros((8, 128), jnp.int32)
    whole = own_tile[...]
    lines = jnp.where(sub == n, own_tile[...], 0)
    for d in range(1, NDIM):
        piece = g1[d]
        line = lax.rem(n + NDIM - d, NDIM)
        lines = jnp.where(sub == line, piece, lines)
        whole = whole + piece
        before = before + jnp.where(line < n, piece, 0)
    tile2[...] = lines
    ints[8:16] = lines
    pl.when(has_low & ~first)(tile_low.start)

    @pl.when(first)
    def _():
        c_in[...] = jnp.zeros((8, 128), jnp.int32)

    pl.when(z > 0)(chain_up.wait_recv)
    c_out[...] = c_in[...] + whole

    @pl.when(z < ZDIM - 1)
    def _():
        pl.semaphore_wait(up_ready, 1)
        chain_up.start()

    pl.when(last)(chain_wrap.start)
    pl.when(has_up)(tile_high.start)
    pl.when(has_up)(pp_high.start)

    prods[0, 0] = mul(a_raw[0, 0], pp[0])
    prods[0, 2] = mul(a_raw[0, 2], pp[1])
    prods[1, 0] = mul(a_raw[1, 0], pp[1])
    prods[1, 1] = mul(a_raw[1, 1], pp[0])

    def transposed(at, block):
        t = block.astype(F32).T.astype(BF)
        pt[at, 0] = t[:B]
        pt[at, 1] = jnp.concatenate([t[256:], t[B:256]], axis=0)

    for r in range(2):
        transposed(r, pp[r])
    pl.when(has_left)(pp_right.wait_recv)
    for r in range(2):
        prods[r, 3] = mul(a_raw[r, 3], pp_s[0, r])
    pl.when(has_right)(pp_left.wait_recv)
    for r in range(2):
        prods[r, 4] = mul(a_raw[r, 4], pp_s[1, r])

    pl.when(has_up)(pp_low.wait_recv)
    pl.when(has_left)(rel_left.start)
    pl.when(has_right)(rel_right.start)
    prods[1, 2] = mul(a_raw[1, 2], pp_up[0])
    pl.when(has_low & ~first)(prod_low.start)
    pl.when(has_up)(tile_low.wait_recv)
    pl.when(has_low & ~first)(tile_rel.start)
    for r in range(2):
        transposed(2 + r, pp_up[r])

    @pl.when(first & has_low)
    def _():
        pl.semaphore_wait(low_ready, 1)
        pp_low.start()
        for q in range(4):
            a_low[q].start()
        one_low.start()
        prod_low.start()
        tile_low.start()
        tile_rel.start()

    @pl.when(first)
    def _():
        chain_wrap.wait_recv()
        for c in totals:
            c.start()
        for c in totals:
            c.wait_recv()
        offset = jnp.zeros((8, 128), jnp.int32)
        for d in range(1, YDIM):
            offset = offset + jnp.where(lax.rem(y + YDIM - d, YDIM) < y, g3[d], 0)
        o_in[...] = offset
        for c in totals:
            c.wait_send()

    @pl.when(first)
    def _():
        o_out[...] = o_in[...]
        chain_two.start()

    def halo(q, xp, x_at, y_at, yp):
        pl.when(has_up)(a_low[q].wait_recv)
        prods[x_at] = mul(a_recv[q, :, :256], rows_first(xp))
        prods[y_at] = mul(a_recv[q, :, 128:], rows_second(yp))

    halo(0, pp_up[0], (2, 0), (2, 1), pp[1])
    halo(1, pp_up[1], (2, 2), (3, 0), pp_up[1])
    pl.when(has_left)(rel_right.wait_recv)
    pl.when(has_right)(rel_left.wait_recv)
    halo(2, pp_su[0, 0], (2, 3), (2, 4), pp_su[1, 0])
    halo(3, pp_su[0, 1], (3, 3), (3, 4), pp_su[1, 1])
    pl.when(has_low)(pp_high.wait_recv)
    pl.when(has_low)(tile_high.wait_recv)
    prods[0, 1] = mul(a_raw[0, 1], pp_dn[...])
    pl.when(has_up)(one_low.wait_recv)
    prods[3, 1] = mul(one_recv[...], pp_up[0])
    pl.when(has_up)(prod_low.wait_recv)
    prods[3, 2] = prod_recv[...]
    pl.when(has_up)(tile_rel.wait_recv)

    @pl.when(z > 0)
    def _():
        chain_two.wait_recv()
        o_out[...] = o_in[...]

    pl.when((z > 0) & ~last)(chain_two.start)
    ints[32:40] = o_out[...] + c_in[...] + before

    for c in gathers:
        c.wait_send()
    pl.when(has_low)(pp_low.wait_send)
    pl.when(has_up)(pp_high.wait_send)
    pl.when(has_left)(pp_left.wait_send)
    pl.when(has_right)(pp_right.wait_send)
    pl.when(has_left)(rel_left.wait_send)
    pl.when(has_right)(rel_right.wait_send)
    for c in a_low:
        pl.when(has_low)(c.wait_send)
    for c in (one_low, prod_low, tile_low, tile_rel):
        pl.when(has_low)(c.wait_send)
    pl.when(has_up)(tile_high.wait_send)
    pl.when(~last)(chain_up.wait_send)
    pl.when(last)(chain_wrap.wait_send)
    pl.when(~last)(chain_two.wait_send)


def gather_all(fine_blocks, prolong_blocks, agg_start):
    vmem = pl.BlockSpec(memory_space=pltpu.VMEM)
    any_ = pl.BlockSpec(memory_space=pl.ANY)
    i8 = pltpu.VMEM((8, 128), jnp.int32)

    def blocks(*lead):
        return pltpu.VMEM(lead + (B, W2), BF)

    dma = pltpu.SemaphoreType.DMA
    return pl.pallas_call(
        exchange_kernel,
        out_shape=(
            jax.ShapeDtypeStruct((4, 5, B, W2), BF),
            jax.ShapeDtypeStruct((4, 2, B, B), BF),
            jax.ShapeDtypeStruct((40, 128), jnp.int32),
        ),
        in_specs=[any_, any_, pl.BlockSpec(memory_space=pltpu.SMEM)],
        out_specs=(vmem, vmem, vmem),
        scratch_shapes=[
            pltpu.VMEM((2, 5, B, B), BF), pltpu.VMEM((2, 2, B, B), BF),
            blocks(2), blocks(2), blocks(), blocks(2, 2), blocks(2, 2),
            blocks(4), blocks(4), pltpu.VMEM((B, B), BF), blocks(),
            i8, pltpu.VMEM((NDIM, 8, 128), jnp.int32), i8, i8, i8, i8, i8, i8,
            pltpu.VMEM((YDIM, 8, 128), jnp.int32), i8,
            dma((2,)), dma((18,)), dma((18,)), dma((NDIM,)), dma((NDIM,)), dma((YDIM,)), dma((YDIM,)),
            pltpu.SemaphoreType.REGULAR, pltpu.SemaphoreType.REGULAR,
        ],
        compiler_params=pltpu.CompilerParams(
            collective_id=7, has_side_effects=True, vmem_limit_bytes=32 << 20),
    )(fine_blocks, prolong_blocks, agg_start)


def terms_kernel(ints, prods, pt, out, numbers, acc):
    w = lax.axis_index("wide")
    n = lax.axis_index("narrow")
    r = pl.program_id(0)
    row = 2 * w + r

    def start_of(line, rel, q):
        at = rel + 2
        line = jnp.clip(line, 0, NDIM - 1)
        return ints[(at // 2) * 8 + line, (at % 2) * 2 + q]

    begins = start_of(n, r, 0) == row
    other = start_of(n, 0, 0) == 2 * w
    rank = ints[32, COUNT_LANE] + jnp.where((r == 1) & other, 1, 0)
    numbers[r] = jnp.where(begins, rank, -1)

    @pl.when(jnp.logical_not(begins))
    def _():
        out[...] = jnp.zeros_like(out)

    @pl.when(begins)
    def _():
        acc[...] = jnp.zeros_like(acc)
        for ahead, p in ((0, 0), (0, 1), (1, 0), (1, 1), (2, 1)):
            i = r + ahead
            matched = (start_of(n, i, p) == row) & (2 * w + i < 2 * WDIM)

            @pl.when(matched)
            def _():
                @pl.loop(0, 5)
                def _(k):
                    line = n + jnp.where(k == 3, -1, jnp.where(k == 4, 1, 0))
                    rel = i + jnp.where(k == 1, -1, jnp.where(k == 2, 1, 0))
                    x = 2 * w + rel
                    there = (line >= 0) & (line < NDIM) & (x >= 0) & (x < 2 * WDIM)
                    base = jnp.where(k == 3, 9, jnp.where(k == 4, 14, 3)) - row

                    @pl.when(there)
                    def _():
                        term = jnp.dot(pt[i, p], prods[i, k], preferred_element_type=F32)
                        c0 = base + start_of(line, rel, 0)
                        c1 = base + start_of(line, rel, 1)

                        @pl.when((c0 >= 0) & (c0 < SLOTS))
                        def _():
                            acc[c0] += term[:, :B]

                        @pl.when((c1 >= 0) & (c1 < SLOTS))
                        def _():
                            acc[c1, :, :128] += term[:, 256:]
                            acc[c1, :, 128:] += term[:, B:256]

        out[0] = acc[...].astype(BF)


def all_terms(ints, prods, pt):
    whole = lambda *shape: pl.BlockSpec(shape, lambda r: (0,) * len(shape))
    smem = pltpu.SMEM
    return pl.pallas_call(
        terms_kernel,
        grid=(2,),
        out_shape=(
            jax.ShapeDtypeStruct((2, SLOTS, B, B), BF),
            jax.ShapeDtypeStruct((2,), jnp.int32),
        ),
        in_specs=[
            pl.BlockSpec(memory_space=smem),
            pl.BlockSpec(memory_space=pltpu.VMEM),
            pl.BlockSpec(memory_space=pltpu.VMEM),
        ],
        out_specs=(
            pl.BlockSpec((1, SLOTS, B, B), lambda r: (r, 0, 0, 0)),
            pl.BlockSpec(memory_space=smem),
        ),
        scratch_shapes=[pltpu.VMEM((SLOTS, B, B), F32)],
        compiler_params=pltpu.CompilerParams(vmem_limit_bytes=32 << 20),
    )(ints, prods, pt)


def per_device(fine_blocks, prolong_blocks, agg_start):
    prods, pt, ints = gather_all(fine_blocks, prolong_blocks, agg_start)
    return all_terms(ints, prods, pt)


def solution(mesh):
    placed = (
        P(("wide", "narrow"), None, None, None),
        P(("wide", "narrow"), None, None, None),
        P(("wide", "narrow"), None),
    )
    return jax.shard_map(
        per_device,
        mesh=mesh,
        in_specs=placed,
        out_specs=(P(("wide", "narrow"), None, None, None), P(("wide", "narrow"))),
        check_vma=False,
    )
```

```python
import functools

import jax
import jax.numpy as jnp
from jax import lax
from jax.experimental import pallas as pl
from jax.experimental.pallas import tpu as pltpu
from jax.sharding import PartitionSpec as P

SLOTS = 17
ZDIM = 16
YDIM = 8
NDIM = 8
WDIM = 128
MID = 7
ROOT = 14
VMEM_LIMIT = 56 << 20
B = 192
W2 = 384
MESH = pl.DeviceIdType.MESH
BF = jnp.bfloat16
F32 = jnp.float32
COUNT_LANE = 4


def pack(x, y):
    lane = lax.broadcasted_iota(jnp.int32, (B, 128), 1)
    xh = jnp.concatenate([x[:, 128:].astype(F32), jnp.zeros((B, 64), F32)], axis=1)
    yh = jnp.concatenate([jnp.zeros((B, 64), F32), y[:, 128:].astype(F32)], axis=1)
    mid = jnp.where(lane < 64, xh, yh).astype(BF)
    return jnp.concatenate([x[:, :128], mid, y[:, :128]], axis=1)


def rows_first(pp):
    return jnp.concatenate([pp, jnp.zeros((64, W2), BF)], axis=0)


def rows_second(pp):
    return jnp.concatenate([jnp.zeros((64, W2), BF), pp[128:], pp[:128]], axis=0)


def mul(a, b):
    return jnp.dot(a, b, preferred_element_type=F32).astype(BF)


def exchange_kernel(
    a_hbm, p_hbm, start_ref,
    prods_hbm, pt_hbm, ints,
    prods, pt, a_raw, p_raw, pp, pp_up, pp_dn, pp_s, pp_su,
    a_send, a_recv, one_recv, prod_recv,
    own_tile, g1, tile2, c_own, g2, t_own, o_in, g3, o_all, c_zero,
    local_sem, out_sem, ssem, rsem, gs, gr, ys, yr, cr, os, up_ready, low_ready, root_ready,
):
    w = lax.axis_index("wide")
    n = lax.axis_index("narrow")
    y = w // ZDIM
    z = w % ZDIM
    has_low = w > 0
    has_up = w < WDIM - 1
    low_w = jnp.maximum(w - 1, 0)
    up_w = jnp.minimum(w + 1, WDIM - 1)
    first = z == 0
    last = z == ZDIM - 1
    root = z == ROOT
    mid = z == MID
    below_mid = (z > 0) & (z < MID)
    root_at = (y * ZDIM + ROOT, n)
    mid_at = (y * ZDIM + MID, n)
    has_left = n > 0
    has_right = n < NDIM - 1
    left = jnp.maximum(n - 1, 0)
    right = jnp.minimum(n + 1, NDIM - 1)

    load_p = pltpu.make_async_copy(p_hbm, p_raw, local_sem.at[0])
    load_a = pltpu.make_async_copy(a_hbm, a_raw, local_sem.at[1])
    load_p.start()
    load_a.start()

    barrier = pltpu.get_barrier_semaphore()

    def greet(dev):
        pl.semaphore_signal(barrier, inc=1, device_id=dev, device_id_type=MESH)

    @pl.when(z < ZDIM - 1)
    def _():
        greet((up_w, n))

    for d in range(1, NDIM):
        greet((w, lax.rem(n + d, NDIM)))

    @pl.when(first & has_low)
    def _():
        greet((low_w, n))

    @pl.when(below_mid & (z < MID - 1))
    def _():
        greet(mid_at)

    @pl.when(z < ROOT - 1)
    def _():
        greet(root_at)

    @pl.when(root)
    def _():
        for d in range(1, YDIM):
            greet((lax.rem(y + d, YDIM) * ZDIM + ROOT, n))

    lane = lax.broadcasted_iota(jnp.int32, (8, 128), 1)
    sub = lax.broadcasted_iota(jnp.int32, (8, 128), 0)
    s00, s01, s10, s11 = (start_ref[i, j] for i in range(2) for j in range(2))
    count = (s00 == 2 * w).astype(jnp.int32) + (s10 == 2 * w + 1).astype(jnp.int32)
    tile = jnp.zeros((8, 128), jnp.int32)
    for at, value in enumerate((s00, s01, s10, s11, count)):
        tile = jnp.where(lane == at, value, tile)
    own_tile[...] = tile

    load_p.wait()
    for r in range(2):
        pp[r] = pack(p_raw[r, 0], p_raw[r, 1])

    heard = (
        NDIM - 1
        + jnp.where(first, 0, 1)
        + jnp.where(mid, MID - 2, 0)
        + jnp.where(root, ROOT - 1 + YDIM - 1, 0)
        + jnp.where(last & has_up, 1, 0)
    )
    pl.semaphore_wait(barrier, heard)

    @pl.when(z > 0)
    def _():
        pl.semaphore_signal(up_ready, inc=1, device_id=(low_w, n), device_id_type=MESH)

    @pl.when(last & has_up)
    def _():
        pl.semaphore_signal(low_ready, inc=1, device_id=(up_w, n), device_id_type=MESH)

    def invite(at):
        pl.semaphore_signal(
            root_ready, inc=1, device_id=(y * ZDIM + at, n), device_id_type=MESH)

    @pl.when(mid)
    def _():
        for at in range(1, MID):
            invite(at)

    @pl.when(root)
    def _():
        for at in range(MID, ROOT):
            invite(at)

    def remote(src, dst, at, dev):
        return pltpu.make_async_remote_copy(
            src_ref=src, dst_ref=dst, send_sem=ssem.at[at], recv_sem=rsem.at[at],
            device_id=dev, device_id_type=MESH)

    low, up = (low_w, n), (up_w, n)
    pp_low = remote(pp, pp_up, 0, low)
    pp_high = remote(pp.at[1], pp_dn, 1, up)
    pp_left = remote(pp, pp_s.at[1], 2, (w, left))
    pp_right = remote(pp, pp_s.at[0], 3, (w, right))
    rel_left = remote(pp_up, pp_su.at[1], 4, (w, left))
    rel_right = remote(pp_up, pp_su.at[0], 5, (w, right))
    a_low = [remote(a_send.at[q], a_recv.at[q], 6 + q, low) for q in range(4)]
    one_low = remote(a_raw.at[1, 1], one_recv, 10, low)
    prod_low = remote(prods.at[1, 2], prod_recv, 11, low)
    tile_low = remote(tile2, ints.at[pl.ds(16, 8)], 12, low)
    tile_high = remote(tile2, ints.at[pl.ds(0, 8)], 13, up)
    tile_rel = remote(ints.at[pl.ds(16, 8)], ints.at[pl.ds(24, 8)], 14, low)
    to_root = pltpu.make_async_remote_copy(
        src_ref=c_own, dst_ref=g2.at[z], send_sem=ssem.at[15], recv_sem=cr.at[z],
        device_id=(y * ZDIM + jnp.where(z < MID, MID, ROOT), n), device_id_type=MESH)
    from_root = remote(o_all.at[0], o_in, 16, root_at)

    zero_root = pltpu.make_async_remote_copy(
        src_ref=c_zero, dst_ref=g2.at[0], send_sem=os.at[0], recv_sem=cr.at[0],
        device_id=mid_at, device_id_type=MESH)

    def reply(at):
        return pltpu.make_async_remote_copy(
            src_ref=o_all.at[at], dst_ref=o_in, send_sem=os.at[at], recv_sem=rsem.at[16],
            device_id=(y * ZDIM + at, n), device_id_type=MESH)

    def arrived(at):
        return pltpu.make_async_remote_copy(
            src_ref=c_own, dst_ref=g2.at[at], send_sem=ssem.at[15], recv_sem=cr.at[at],
            device_id=root_at, device_id_type=MESH)

    others = [at for at in range(ZDIM) if at != ROOT]
    others = others[ROOT:] + others[:ROOT]
    half = pl.ds(0, MID + 1)
    mid_root = pltpu.make_async_remote_copy(
        src_ref=g2.at[half], dst_ref=g2.at[half], send_sem=os.at[0],
        recv_sem=rsem.at[17], device_id=root_at, device_id_type=MESH)

    gathers = []
    for d in range(1, NDIM):
        gathers.append(pltpu.make_async_remote_copy(
            src_ref=own_tile, dst_ref=g1.at[d], send_sem=gs.at[d], recv_sem=gr.at[d],
            device_id=(w, lax.rem(n + d, NDIM)), device_id_type=MESH))
    totals = []
    for d in range(1, YDIM):
        totals.append(pltpu.make_async_remote_copy(
            src_ref=t_own, dst_ref=g3.at[d], send_sem=ys.at[d], recv_sem=yr.at[d],
            device_id=(lax.rem(y + d, YDIM) * ZDIM + ROOT, n), device_id_type=MESH))

    for c in gathers:
        c.start()
    pl.when(has_low & ~first & ~last)(pp_low.start)
    pl.when(has_left)(pp_left.start)
    pl.when(has_right)(pp_right.start)

    load_a.wait()
    for q, ((i0, k0), (i1, k1)) in enumerate(
        (((0, 0), (0, 1)), ((0, 2), (1, 0)), ((0, 3), (0, 4)), ((1, 3), (1, 4)))):
        a_send[q] = pack(a_raw[i0, k0], a_raw[i1, k1])

    @pl.when(jnp.logical_not(has_up))
    def _():
        pp_up[...] = jnp.zeros_like(pp_up)
        a_recv[...] = jnp.zeros_like(a_recv)
        one_recv[...] = jnp.zeros_like(one_recv)
        prod_recv[...] = jnp.zeros_like(prod_recv)
        ints[16:32] = jnp.zeros((16, 128), jnp.int32)

    @pl.when(jnp.logical_not(has_low))
    def _():
        pp_dn[...] = jnp.zeros_like(pp_dn)
        ints[0:8] = jnp.zeros((8, 128), jnp.int32)

    for side, there in ((0, has_left), (1, has_right)):
        @pl.when(jnp.logical_not(there))
        def _():
            pp_s[side] = jnp.zeros((2, B, W2), BF)
            pp_su[side] = jnp.zeros((2, B, W2), BF)

    for c in gathers:
        c.wait_recv()
    g1[0] = own_tile[...]
    before = jnp.zeros((8, 128), jnp.int32)
    whole = own_tile[...]
    lines = jnp.where(sub == n, own_tile[...], 0)
    for d in range(1, NDIM):
        piece = g1[d]
        line = lax.rem(n + NDIM - d, NDIM)
        lines = jnp.where(sub == line, piece, lines)
        whole = whole + piece
        before = before + jnp.where(line < n, piece, 0)
    tile2[...] = lines
    ints[8:16] = lines
    c_own[...] = whole
    pl.when(z > ROOT)(to_root.start)
    pl.when(last)(pp_low.start)

    @pl.when(has_low & ~first)
    def _():
        tile_low.start()
        for q in range(4):
            a_low[q].start()
        one_low.start()

    @pl.when(~last)
    def _():
        pl.semaphore_wait(up_ready, 1)

    pl.when(has_up)(tile_high.start)
    pl.when(has_up)(pp_high.start)

    stores = [
        pltpu.make_async_copy(prods.at[i, k], prods_hbm.at[i, k], out_sem.at[5 * i + k])
        for i in range(4) for k in range(5)]
    stores.append(pltpu.make_async_copy(pt, pt_hbm, out_sem.at[20]))

    def keep(i, k, value):
        prods[i, k] = value
        stores[5 * i + k].start()

    keep(0, 0, mul(a_raw[0, 0], pp[0]))
    keep(0, 2, mul(a_raw[0, 2], pp[1]))
    keep(1, 0, mul(a_raw[1, 0], pp[1]))
    keep(1, 1, mul(a_raw[1, 1], pp[0]))

    def transposed(at, block):
        t = block.astype(F32).T.astype(BF)
        pt[at, 0] = t[:B]
        pt[at, 1] = jnp.concatenate([t[256:], t[B:256]], axis=0)

    for r in range(2):
        transposed(r, pp[r])
    pl.when(has_left)(pp_right.wait_recv)
    for r in range(2):
        keep(r, 3, mul(a_raw[r, 3], pp_s[0, r]))
    pl.when(has_right)(pp_left.wait_recv)
    for r in range(2):
        keep(r, 4, mul(a_raw[r, 4], pp_s[1, r]))

    @pl.when(z == 1)
    def _():
        tile_high.wait_recv()
        c_zero[...] = jnp.broadcast_to(jnp.sum(ints[0:8], axis=0, keepdims=True), (8, 128))

    @pl.when((z > 0) & (z < ROOT))
    def _():
        pl.semaphore_wait(root_ready, 1)

    pl.when((z > 0) & (z < ROOT) & ~mid)(to_root.start)
    pl.when(z == 1)(zero_root.start)

    @pl.when(mid)
    def _():
        g2[MID] = c_own[...]
        for at in range(MID):
            arrived(at).wait_recv()
        mid_root.start()

    @pl.when(root)
    def _():
        g2[ROOT] = c_own[...]
        mid_root.wait_recv()
        for at in range(MID + 1, ZDIM):
            if at != ROOT:
                arrived(at).wait_recv()
        total = jnp.zeros((8, 128), jnp.int32)
        for at in range(ZDIM):
            o_all[at] = total
            total = total + g2[at]
        t_own[...] = total
        for c in totals:
            c.start()
        for c in totals:
            c.wait_recv()
        offset = jnp.zeros((8, 128), jnp.int32)
        for d in range(1, YDIM):
            offset = offset + jnp.where(lax.rem(y + YDIM - d, YDIM) < y, g3[d], 0)
        for at in range(ZDIM):
            o_all[at] = o_all[at] + offset
        o_in[...] = o_all[ROOT]
        for at in others:
            reply(at).start()

    pl.when(has_up)(pp_low.wait_recv)
    pl.when(has_left)(rel_left.start)
    pl.when(has_right)(rel_right.start)
    keep(1, 2, mul(a_raw[1, 2], pp_up[0]))
    pl.when(has_low & ~first)(prod_low.start)
    pl.when(has_up)(tile_low.wait_recv)
    pl.when(has_low & ~first)(tile_rel.start)
    for r in range(2):
        transposed(2 + r, pp_up[r])
    stores[20].start()

    @pl.when(first & has_low)
    def _():
        pl.semaphore_wait(low_ready, 1)
        pp_low.start()
        tile_low.start()
        for q in range(4):
            a_low[q].start()
        one_low.start()
        prod_low.start()
        tile_rel.start()

    def halo(q, xp, x_at, y_at, yp):
        pl.when(has_up)(a_low[q].wait_recv)
        keep(*x_at, mul(a_recv[q, :, :256], rows_first(xp)))
        keep(*y_at, mul(a_recv[q, :, 128:], rows_second(yp)))

    halo(0, pp_up[0], (2, 0), (2, 1), pp[1])
    halo(1, pp_up[1], (2, 2), (3, 0), pp_up[1])
    pl.when(has_left)(rel_right.wait_recv)
    pl.when(has_right)(rel_left.wait_recv)
    halo(2, pp_su[0, 0], (2, 3), (2, 4), pp_su[1, 0])
    halo(3, pp_su[0, 1], (3, 3), (3, 4), pp_su[1, 1])
    pl.when(has_low)(pp_high.wait_recv)
    pl.when(has_low & (z != 1))(tile_high.wait_recv)
    keep(0, 1, mul(a_raw[0, 1], pp_dn[...]))
    pl.when(has_up)(one_low.wait_recv)
    keep(3, 1, mul(one_recv[...], pp_up[0]))
    pl.when(has_up)(prod_low.wait_recv)
    keep(3, 2, prod_recv[...])
    pl.when(has_up)(tile_rel.wait_recv)

    pl.when(~root)(from_root.wait_recv)
    ints[32:40] = o_in[...] + before

    for c in gathers:
        c.wait_send()
    pl.when(has_low)(pp_low.wait_send)
    pl.when(has_up)(pp_high.wait_send)
    pl.when(has_left)(pp_left.wait_send)
    pl.when(has_right)(pp_right.wait_send)
    pl.when(has_left)(rel_left.wait_send)
    pl.when(has_right)(rel_right.wait_send)
    for c in a_low:
        pl.when(has_low)(c.wait_send)
    for c in (one_low, prod_low, tile_low, tile_rel):
        pl.when(has_low)(c.wait_send)
    pl.when(has_up)(tile_high.wait_send)
    pl.when(~root & ~first & ~mid)(to_root.wait_send)
    pl.when(mid)(mid_root.wait_send)
    pl.when(z == 1)(zero_root.wait_send)

    @pl.when(root)
    def _():
        for c in totals:
            c.wait_send()
        for at in others:
            reply(at).wait_send()

    for c in stores:
        c.wait()


def gather_all(fine_blocks, prolong_blocks, agg_start):
    vmem = pl.BlockSpec(memory_space=pltpu.VMEM)
    any_ = pl.BlockSpec(memory_space=pl.ANY)
    i8 = pltpu.VMEM((8, 128), jnp.int32)

    def blocks(*lead):
        return pltpu.VMEM(lead + (B, W2), BF)

    def tiles(count):
        return pltpu.VMEM((count, 8, 128), jnp.int32)

    dma = pltpu.SemaphoreType.DMA
    regular = pltpu.SemaphoreType.REGULAR
    return pl.pallas_call(
        exchange_kernel,
        out_shape=(
            jax.ShapeDtypeStruct((4, 5, B, W2), BF),
            jax.ShapeDtypeStruct((4, 2, B, B), BF),
            jax.ShapeDtypeStruct((40, 128), jnp.int32),
        ),
        in_specs=[any_, any_, pl.BlockSpec(memory_space=pltpu.SMEM)],
        out_specs=(any_, any_, vmem),
        scratch_shapes=[
            blocks(4, 5), pltpu.VMEM((4, 2, B, B), BF),
            pltpu.VMEM((2, 5, B, B), BF), pltpu.VMEM((2, 2, B, B), BF),
            blocks(2), blocks(2), blocks(), blocks(2, 2), blocks(2, 2),
            blocks(4), blocks(4), pltpu.VMEM((B, B), BF), blocks(),
            i8, tiles(NDIM), i8, i8, tiles(ZDIM), i8, i8, tiles(YDIM), tiles(ZDIM), i8,
            dma((2,)), dma((21,)), dma((17,)), dma((18,)), dma((NDIM,)), dma((NDIM,)),
            dma((YDIM,)), dma((YDIM,)), dma((ZDIM,)), dma((ZDIM,)),
            regular, regular, regular,
        ],
        compiler_params=pltpu.CompilerParams(
            collective_id=7, has_side_effects=True, vmem_limit_bytes=VMEM_LIMIT),
    )(fine_blocks, prolong_blocks, agg_start)


def terms_kernel(ints, prods_hbm, pt_hbm, out_hbm, numbers, prods, pt, acc, out, in_sem, out_sem):
    w = lax.axis_index("wide")
    n = lax.axis_index("narrow")
    loads = [
        pltpu.make_async_copy(prods_hbm.at[i], prods.at[i], in_sem.at[i]) for i in range(4)]
    load_pt = pltpu.make_async_copy(pt_hbm, pt, in_sem.at[4])
    load_pt.start()
    for c in loads:
        c.start()

    def start_of(line, rel, q):
        at = rel + 2
        line = jnp.clip(line, 0, NDIM - 1)
        return ints[(at // 2) * 8 + line, (at % 2) * 2 + q]

    other = start_of(n, 0, 0) == 2 * w
    for r in range(2):
        row = 2 * w + r
        begins = start_of(n, r, 0) == row
        rank = ints[32, COUNT_LANE]
        if r == 1:
            rank = rank + jnp.where(other, 1, 0)
        numbers[r] = jnp.where(begins, rank, -1)

        def add(i, columns, row=row, r=r):
            for k in range(5):
                line = n + (0, 0, 0, -1, 1)[k]
                rel = i + (0, -1, 1, 0, 0)[k]
                x = 2 * w + rel
                there = (line >= 0) & (line < NDIM) & (x >= 0) & (x < 2 * WDIM)
                base = (3, 3, 3, 9, 14)[k] - row
                slots = []
                for q in range(2):
                    c = base + start_of(line, rel, q)
                    slots.append(jnp.where(there & (c >= 0) & (c < SLOTS), c, SLOTS))
                term = sum(
                    jnp.dot(pt[i, p], prods[i, k], preferred_element_type=F32)
                    for p in columns)
                acc[r, slots[0]] += term[:, :B]
                acc[r, slots[1], :, :128] += term[:, 256:]
                acc[r, slots[1], :, 128:] += term[:, B:256]

        acc[r] = jnp.zeros((SLOTS + 1, B, B), F32)
        if r == 0:
            load_pt.wait()
        for ahead in range(3):
            i = r + ahead
            if r == 0 or ahead == 2:
                loads[i].wait()
            inside = begins & (2 * w + i < 2 * WDIM)
            first = inside & (start_of(n, i, 0) == row)
            second = inside & (start_of(n, i, 1) == row)
            if ahead == 2:
                pl.when(second)(functools.partial(add, i, (1,)))
            else:
                pl.when(first & second)(functools.partial(add, i, (0, 1)))
                pl.when(first & ~second)(functools.partial(add, i, (0,)))
                pl.when(second & ~first)(functools.partial(add, i, (1,)))
        out[r] = acc[r, :SLOTS].astype(BF)
        pltpu.make_async_copy(out.at[r], out_hbm.at[r], out_sem.at[r]).start()
    for r in range(2):
        pltpu.make_async_copy(out.at[r], out_hbm.at[r], out_sem.at[r]).wait()


def all_terms(ints, prods, pt):
    any_ = pl.BlockSpec(memory_space=pl.ANY)
    smem = pl.BlockSpec(memory_space=pltpu.SMEM)
    return pl.pallas_call(
        terms_kernel,
        out_shape=(
            jax.ShapeDtypeStruct((2, SLOTS, B, B), BF),
            jax.ShapeDtypeStruct((2,), jnp.int32),
        ),
        in_specs=[smem, any_, any_],
        out_specs=(any_, smem),
        scratch_shapes=[
            pltpu.VMEM((4, 5, B, W2), BF), pltpu.VMEM((4, 2, B, B), BF),
            pltpu.VMEM((2, SLOTS + 1, B, B), F32), pltpu.VMEM((2, SLOTS, B, B), BF),
            pltpu.SemaphoreType.DMA((5,)), pltpu.SemaphoreType.DMA((2,)),
        ],
        compiler_params=pltpu.CompilerParams(vmem_limit_bytes=VMEM_LIMIT),
    )(ints, prods, pt)


def per_device(fine_blocks, prolong_blocks, agg_start):
    prods, pt, ints = gather_all(fine_blocks, prolong_blocks, agg_start)
    return all_terms(ints, prods, pt)


def solution(mesh):
    placed = (
        P(("wide", "narrow"), None, None, None),
        P(("wide", "narrow"), None, None, None),
        P(("wide", "narrow"), None),
    )
    return jax.shard_map(
        per_device,
        mesh=mesh,
        in_specs=placed,
        out_specs=(P(("wide", "narrow"), None, None, None), P(("wide", "narrow"))),
        check_vma=False,
    )
```

```python
import functools

import jax
import jax.numpy as jnp
from jax import lax
from jax.experimental import pallas as pl
from jax.experimental.pallas import tpu as pltpu
from jax.sharding import PartitionSpec as P

SLOTS = 17
ZDIM = 16
YDIM = 8
NDIM = 8
WDIM = 128
MID = 7
ROOT = 14
VMEM_LIMIT = 56 << 20
B = 192
W2 = 384
MESH = pl.DeviceIdType.MESH
BF = jnp.bfloat16
F32 = jnp.float32
COUNT_LANE = 4


def pack(x, y):
    lane = lax.broadcasted_iota(jnp.int32, (B, 128), 1)
    xh = jnp.concatenate([x[:, 128:].astype(F32), jnp.zeros((B, 64), F32)], axis=1)
    yh = jnp.concatenate([jnp.zeros((B, 64), F32), y[:, 128:].astype(F32)], axis=1)
    mid = jnp.where(lane < 64, xh, yh).astype(BF)
    return jnp.concatenate([x[:, :128], mid, y[:, :128]], axis=1)


def rows_first(pp):
    return jnp.concatenate([pp, jnp.zeros((64, W2), BF)], axis=0)


def rows_second(pp):
    return jnp.concatenate([jnp.zeros((64, W2), BF), pp[128:], pp[:128]], axis=0)


def mul(a, b):
    return jnp.dot(a, b, preferred_element_type=F32).astype(BF)


def exchange_kernel(
    a_hbm, p_hbm, start_ref,
    out_hbm, numbers,
    ints, prods, pt, acc, out, rank_tile, rank_smem, a_raw, p_raw, pp, pp_up, pp_dn, pp_s, pp_su,
    a_send, a_recv, one_recv, prod_recv,
    own_tile, g1, tile2, c_own, g2, t_own, o_in, g3, o_all, c_zero,
    local_sem, out_sem, ssem, rsem, gs, gr, ys, yr, cr, os, up_ready, low_ready, root_ready,
):
    w = lax.axis_index("wide")
    n = lax.axis_index("narrow")
    y = w // ZDIM
    z = w % ZDIM
    has_low = w > 0
    has_up = w < WDIM - 1
    low_w = jnp.maximum(w - 1, 0)
    up_w = jnp.minimum(w + 1, WDIM - 1)
    first = z == 0
    last = z == ZDIM - 1
    root = z == ROOT
    mid = z == MID
    below_mid = (z > 0) & (z < MID)
    root_at = (y * ZDIM + ROOT, n)
    mid_at = (y * ZDIM + MID, n)
    has_left = n > 0
    has_right = n < NDIM - 1
    left = jnp.maximum(n - 1, 0)
    right = jnp.minimum(n + 1, NDIM - 1)

    load_p = pltpu.make_async_copy(p_hbm, p_raw, local_sem.at[0])
    load_a = pltpu.make_async_copy(a_hbm, a_raw, local_sem.at[1])
    load_p.start()
    load_a.start()

    barrier = pltpu.get_barrier_semaphore()

    def greet(dev):
        pl.semaphore_signal(barrier, inc=1, device_id=dev, device_id_type=MESH)

    @pl.when(z < ZDIM - 1)
    def _():
        greet((up_w, n))

    for d in range(1, NDIM):
        greet((w, lax.rem(n + d, NDIM)))

    @pl.when(first & has_low)
    def _():
        greet((low_w, n))

    @pl.when(below_mid & (z < MID - 1))
    def _():
        greet(mid_at)

    @pl.when(z < ROOT - 1)
    def _():
        greet(root_at)

    @pl.when(root)
    def _():
        for d in range(1, YDIM):
            greet((lax.rem(y + d, YDIM) * ZDIM + ROOT, n))

    lane = lax.broadcasted_iota(jnp.int32, (8, 128), 1)
    sub = lax.broadcasted_iota(jnp.int32, (8, 128), 0)
    s00, s01, s10, s11 = (start_ref[i, j] for i in range(2) for j in range(2))
    count = (s00 == 2 * w).astype(jnp.int32) + (s10 == 2 * w + 1).astype(jnp.int32)
    tile = jnp.zeros((8, 128), jnp.int32)
    for at, value in enumerate((s00, s01, s10, s11, count)):
        tile = jnp.where(lane == at, value, tile)
    own_tile[...] = tile

    heard = (
        NDIM - 1
        + jnp.where(first, 0, 1)
        + jnp.where(mid, MID - 2, 0)
        + jnp.where(root, ROOT - 1 + YDIM - 1, 0)
        + jnp.where(last & has_up, 1, 0)
    )
    pl.semaphore_wait(barrier, heard)

    @pl.when(z > 0)
    def _():
        pl.semaphore_signal(up_ready, inc=1, device_id=(low_w, n), device_id_type=MESH)

    @pl.when(last & has_up)
    def _():
        pl.semaphore_signal(low_ready, inc=1, device_id=(up_w, n), device_id_type=MESH)

    def invite(at):
        pl.semaphore_signal(
            root_ready, inc=1, device_id=(y * ZDIM + at, n), device_id_type=MESH)

    @pl.when(mid)
    def _():
        for at in range(1, MID):
            invite(at)

    @pl.when(root)
    def _():
        for at in range(MID, ROOT):
            invite(at)

    load_p.wait()
    for r in range(2):
        pp[r] = pack(p_raw[r, 0], p_raw[r, 1])

    def remote(src, dst, at, dev):
        return pltpu.make_async_remote_copy(
            src_ref=src, dst_ref=dst, send_sem=ssem.at[at], recv_sem=rsem.at[at],
            device_id=dev, device_id_type=MESH)

    low, up = (low_w, n), (up_w, n)
    pp_low = remote(pp, pp_up, 0, low)
    pp_high = remote(pp.at[1], pp_dn, 1, up)
    pp_left = remote(pp, pp_s.at[1], 2, (w, left))
    pp_right = remote(pp, pp_s.at[0], 3, (w, right))
    rel_left = remote(pp_up, pp_su.at[1], 4, (w, left))
    rel_right = remote(pp_up, pp_su.at[0], 5, (w, right))
    a_low = [remote(a_send.at[q], a_recv.at[q], 6 + q, low) for q in range(4)]
    one_low = remote(a_raw.at[1, 1], one_recv, 10, low)
    prod_low = remote(prods.at[1, 2], prod_recv, 11, low)
    tile_low = remote(tile2, ints.at[pl.ds(16, 8)], 12, low)
    tile_high = remote(tile2, ints.at[pl.ds(0, 8)], 13, up)
    tile_rel = remote(ints.at[pl.ds(16, 8)], ints.at[pl.ds(24, 8)], 14, low)
    to_root = pltpu.make_async_remote_copy(
        src_ref=c_own, dst_ref=g2.at[z], send_sem=ssem.at[15], recv_sem=cr.at[z],
        device_id=(y * ZDIM + jnp.where(z < MID, MID, ROOT), n), device_id_type=MESH)
    from_root = remote(o_all.at[0], o_in, 16, root_at)

    zero_root = pltpu.make_async_remote_copy(
        src_ref=c_zero, dst_ref=g2.at[0], send_sem=os.at[0], recv_sem=cr.at[0],
        device_id=mid_at, device_id_type=MESH)

    def reply(at):
        return pltpu.make_async_remote_copy(
            src_ref=o_all.at[at], dst_ref=o_in, send_sem=os.at[at], recv_sem=rsem.at[16],
            device_id=(y * ZDIM + at, n), device_id_type=MESH)

    def arrived(at):
        return pltpu.make_async_remote_copy(
            src_ref=c_own, dst_ref=g2.at[at], send_sem=ssem.at[15], recv_sem=cr.at[at],
            device_id=root_at, device_id_type=MESH)

    others = [at for at in range(ZDIM) if at != ROOT]
    others = others[ROOT:] + others[:ROOT]
    half = pl.ds(0, MID + 1)
    mid_root = pltpu.make_async_remote_copy(
        src_ref=g2.at[half], dst_ref=g2.at[half], send_sem=os.at[0],
        recv_sem=rsem.at[17], device_id=root_at, device_id_type=MESH)

    gathers = []
    for d in range(1, NDIM):
        gathers.append(pltpu.make_async_remote_copy(
            src_ref=own_tile, dst_ref=g1.at[d], send_sem=gs.at[d], recv_sem=gr.at[d],
            device_id=(w, lax.rem(n + d, NDIM)), device_id_type=MESH))
    totals = []
    for d in range(1, YDIM):
        totals.append(pltpu.make_async_remote_copy(
            src_ref=t_own, dst_ref=g3.at[d], send_sem=ys.at[d], recv_sem=yr.at[d],
            device_id=(lax.rem(y + d, YDIM) * ZDIM + ROOT, n), device_id_type=MESH))

    for c in gathers:
        c.start()
    pl.when(has_low & ~first & ~last)(pp_low.start)
    pl.when(has_left)(pp_left.start)
    pl.when(has_right)(pp_right.start)

    load_a.wait()
    for q, ((i0, k0), (i1, k1)) in enumerate(
        (((0, 0), (0, 1)), ((0, 2), (1, 0)), ((0, 3), (0, 4)), ((1, 3), (1, 4)))):
        a_send[q] = pack(a_raw[i0, k0], a_raw[i1, k1])

    @pl.when(jnp.logical_not(has_up))
    def _():
        pp_up[...] = jnp.zeros_like(pp_up)
        a_recv[...] = jnp.zeros_like(a_recv)
        one_recv[...] = jnp.zeros_like(one_recv)
        prod_recv[...] = jnp.zeros_like(prod_recv)
        ints[16:32] = jnp.zeros((16, 128), jnp.int32)

    @pl.when(jnp.logical_not(has_low))
    def _():
        pp_dn[...] = jnp.zeros_like(pp_dn)
        ints[0:8] = jnp.zeros((8, 128), jnp.int32)

    for side, there in ((0, has_left), (1, has_right)):
        @pl.when(jnp.logical_not(there))
        def _():
            pp_s[side] = jnp.zeros((2, B, W2), BF)
            pp_su[side] = jnp.zeros((2, B, W2), BF)

    for c in gathers:
        c.wait_recv()
    g1[0] = own_tile[...]
    before = jnp.zeros((8, 128), jnp.int32)
    whole = own_tile[...]
    lines = jnp.where(sub == n, own_tile[...], 0)
    for d in range(1, NDIM):
        piece = g1[d]
        line = lax.rem(n + NDIM - d, NDIM)
        lines = jnp.where(sub == line, piece, lines)
        whole = whole + piece
        before = before + jnp.where(line < n, piece, 0)
    tile2[...] = lines
    ints[8:16] = lines
    c_own[...] = whole
    pl.when(z > ROOT)(to_root.start)
    pl.when(last)(pp_low.start)

    @pl.when(has_low & ~first)
    def _():
        tile_low.start()
        for q in range(4):
            a_low[q].start()
        one_low.start()

    @pl.when(~last)
    def _():
        pl.semaphore_wait(up_ready, 1)

    pl.when(has_up)(tile_high.start)
    pl.when(has_up)(pp_high.start)

    def keep(i, k, value):
        prods[i, k] = value

    keep(0, 0, mul(a_raw[0, 0], pp[0]))
    keep(0, 2, mul(a_raw[0, 2], pp[1]))
    keep(1, 0, mul(a_raw[1, 0], pp[1]))
    keep(1, 1, mul(a_raw[1, 1], pp[0]))

    def transposed(at, block):
        t = block.astype(F32).T.astype(BF)
        pt[at, 0] = t[:B]
        pt[at, 1] = jnp.concatenate([t[256:], t[B:256]], axis=0)

    for r in range(2):
        transposed(r, pp[r])
    pl.when(has_left)(pp_right.wait_recv)
    for r in range(2):
        keep(r, 3, mul(a_raw[r, 3], pp_s[0, r]))
    pl.when(has_right)(pp_left.wait_recv)
    for r in range(2):
        keep(r, 4, mul(a_raw[r, 4], pp_s[1, r]))

    @pl.when(z == 1)
    def _():
        tile_high.wait_recv()
        c_zero[...] = jnp.broadcast_to(jnp.sum(ints[0:8], axis=0, keepdims=True), (8, 128))

    @pl.when((z > 0) & (z < ROOT))
    def _():
        pl.semaphore_wait(root_ready, 1)

    pl.when((z > 0) & (z < ROOT) & ~mid)(to_root.start)
    pl.when(z == 1)(zero_root.start)

    @pl.when(mid)
    def _():
        g2[MID] = c_own[...]
        for at in range(MID):
            arrived(at).wait_recv()
        mid_root.start()

    @pl.when(root)
    def _():
        g2[ROOT] = c_own[...]
        mid_root.wait_recv()
        for at in range(MID + 1, ZDIM):
            if at != ROOT:
                arrived(at).wait_recv()
        total = jnp.zeros((8, 128), jnp.int32)
        for at in range(ZDIM):
            o_all[at] = total
            total = total + g2[at]
        t_own[...] = total
        for c in totals:
            c.start()
        for c in totals:
            c.wait_recv()
        offset = jnp.zeros((8, 128), jnp.int32)
        for d in range(1, YDIM):
            offset = offset + jnp.where(lax.rem(y + YDIM - d, YDIM) < y, g3[d], 0)
        for at in range(ZDIM):
            o_all[at] = o_all[at] + offset
        o_in[...] = o_all[ROOT]
        for at in others:
            reply(at).start()

    pl.when(has_up)(pp_low.wait_recv)
    pl.when(has_left)(rel_left.start)
    pl.when(has_right)(rel_right.start)
    keep(1, 2, mul(a_raw[1, 2], pp_up[0]))
    pl.when(has_low & ~first)(prod_low.start)
    pl.when(has_up)(tile_low.wait_recv)
    pl.when(has_low & ~first)(tile_rel.start)
    for r in range(2):
        transposed(2 + r, pp_up[r])

    @pl.when(first & has_low)
    def _():
        pl.semaphore_wait(low_ready, 1)
        pp_low.start()
        tile_low.start()
        for q in range(4):
            a_low[q].start()
        one_low.start()
        prod_low.start()
        tile_rel.start()

    def halo(q, xp, x_at, y_at, yp):
        pl.when(has_up)(a_low[q].wait_recv)
        keep(*x_at, mul(a_recv[q, :, :256], rows_first(xp)))
        keep(*y_at, mul(a_recv[q, :, 128:], rows_second(yp)))

    halo(0, pp_up[0], (2, 0), (2, 1), pp[1])
    halo(1, pp_up[1], (2, 2), (3, 0), pp_up[1])
    pl.when(has_left)(rel_right.wait_recv)
    pl.when(has_right)(rel_left.wait_recv)
    halo(2, pp_su[0, 0], (2, 3), (2, 4), pp_su[1, 0])
    halo(3, pp_su[0, 1], (3, 3), (3, 4), pp_su[1, 1])
    pl.when(has_low)(pp_high.wait_recv)
    pl.when(has_low & (z != 1))(tile_high.wait_recv)
    keep(0, 1, mul(a_raw[0, 1], pp_dn[...]))
    pl.when(has_up)(one_low.wait_recv)
    keep(3, 1, mul(one_recv[...], pp_up[0]))
    pl.when(has_up)(prod_low.wait_recv)
    keep(3, 2, prod_recv[...])
    pl.when(has_up)(tile_rel.wait_recv)

    def start_of(line, rel, q):
        tile = ints[(rel + 2) // 2 * 8:(rel + 2) // 2 * 8 + 8]
        at = (rel % 2) * 2 + q
        chosen = jnp.where((sub == line) & (lane == at), tile, 0)
        return jnp.sum(jnp.sum(chosen, axis=1, keepdims=True), axis=0, keepdims=True)

    starts = {}
    for rel in range(-1, 5):
        for side in (-1, 0, 1) if 0 <= rel < 4 else (0,):
            for q in range(2):
                starts[rel, side, q] = start_of(n + side, rel, q)

    stores = []
    for r in range(2):
        acc[...] = jnp.zeros_like(acc)
        for ahead in range(3):
            i = r + ahead
            inside = 2 * w + i < 2 * WDIM
            left_sides = []
            for p in (1,) if ahead == 2 else (0, 1):
                mine = (starts[i, 0, p] == 2 * w + r) & inside
                chosen = jnp.where(mine, pt[i, p].astype(F32), 0.0).astype(BF)
                left_sides.append(chosen)
            for k in range(5):
                side = (0, 0, 0, -1, 1)[k]
                rel = i + (0, -1, 1, 0, 0)[k]
                x = 2 * w + rel
                there = (n + side >= 0) & (n + side < NDIM) & (x >= 0) & (x < 2 * WDIM)
                term = sum(
                    jnp.dot(c, prods[i, k], preferred_element_type=F32) for c in left_sides)

                def put(q, shift, r=r, k=k, rel=rel, there=there, term=term, side=side, x=x):
                    slot = (3, 3, 3, 9, 14)[k] + rel + shift - r
                    here = (starts[rel, side, q] == x + shift) & there
                    if q == 0:
                        acc[slot] += jnp.where(here, term[:, :B], 0.0)
                    else:
                        acc[slot, :, :128] += jnp.where(here, term[:, 256:], 0.0)
                        acc[slot, :, 128:] += jnp.where(here, term[:, B:256], 0.0)

                put(0, 0)
                put(0, -1)
                put(1, -1)
                put(1, -2)
                if rel == 0:
                    pl.when(w == 0)(functools.partial(put, 1, 0))
        out[r] = acc[...].astype(BF)
        stores.append(pltpu.make_async_copy(out.at[r], out_hbm.at[r], out_sem.at[r]))
        stores[r].start()

    pl.when(~root)(from_root.wait_recv)
    rank_tile[...] = o_in[...] + before
    ranks = pltpu.make_async_copy(rank_tile, rank_smem, local_sem.at[0])
    ranks.start()
    ranks.wait()
    rank = rank_smem[0, COUNT_LANE]
    begins = s00 == 2 * w
    numbers[0] = jnp.where(begins, rank, -1)
    numbers[1] = jnp.where(s10 == 2 * w + 1, rank + jnp.where(begins, 1, 0), -1)

    for c in gathers:
        c.wait_send()
    pl.when(has_low)(pp_low.wait_send)
    pl.when(has_up)(pp_high.wait_send)
    pl.when(has_left)(pp_left.wait_send)
    pl.when(has_right)(pp_right.wait_send)
    pl.when(has_left)(rel_left.wait_send)
    pl.when(has_right)(rel_right.wait_send)
    for c in a_low:
        pl.when(has_low)(c.wait_send)
    for c in (one_low, prod_low, tile_low, tile_rel):
        pl.when(has_low)(c.wait_send)
    pl.when(has_up)(tile_high.wait_send)
    pl.when(~root & ~first & ~mid)(to_root.wait_send)
    pl.when(mid)(mid_root.wait_send)
    pl.when(z == 1)(zero_root.wait_send)

    @pl.when(root)
    def _():
        for c in totals:
            c.wait_send()
        for at in others:
            reply(at).wait_send()

    for c in stores:
        c.wait()


def gather_all(fine_blocks, prolong_blocks, agg_start):
    smem = pl.BlockSpec(memory_space=pltpu.SMEM)
    any_ = pl.BlockSpec(memory_space=pl.ANY)
    i8 = pltpu.VMEM((8, 128), jnp.int32)

    def blocks(*lead):
        return pltpu.VMEM(lead + (B, W2), BF)

    def tiles(count):
        return pltpu.VMEM((count, 8, 128), jnp.int32)

    dma = pltpu.SemaphoreType.DMA
    regular = pltpu.SemaphoreType.REGULAR
    return pl.pallas_call(
        exchange_kernel,
        out_shape=(
            jax.ShapeDtypeStruct((2, SLOTS, B, B), BF),
            jax.ShapeDtypeStruct((2,), jnp.int32),
        ),
        in_specs=[any_, any_, smem],
        out_specs=(any_, smem),
        scratch_shapes=[
            pltpu.VMEM((32, 128), jnp.int32),
            blocks(4, 5), pltpu.VMEM((4, 2, B, B), BF),
            pltpu.VMEM((SLOTS, B, B), F32), pltpu.VMEM((2, SLOTS, B, B), BF),
            i8, pltpu.SMEM((8, 128), jnp.int32),
            pltpu.VMEM((2, 5, B, B), BF), pltpu.VMEM((2, 2, B, B), BF),
            blocks(2), blocks(2), blocks(), blocks(2, 2), blocks(2, 2),
            blocks(4), blocks(4), pltpu.VMEM((B, B), BF), blocks(),
            i8, tiles(NDIM), i8, i8, tiles(ZDIM), i8, i8, tiles(YDIM), tiles(ZDIM), i8,
            dma((2,)), dma((2,)), dma((17,)), dma((18,)), dma((NDIM,)), dma((NDIM,)),
            dma((YDIM,)), dma((YDIM,)), dma((ZDIM,)), dma((ZDIM,)),
            regular, regular, regular,
        ],
        compiler_params=pltpu.CompilerParams(
            collective_id=7, has_side_effects=True, vmem_limit_bytes=VMEM_LIMIT),
    )(fine_blocks, prolong_blocks, agg_start)


def hand_over_kernel(blocks_hbm, numbers_hbm, out_hbm, out_numbers, held, in_sem, out_sem):
    copies = [(r, slice(at, min(at + 3, SLOTS))) for r in range(2) for at in range(0, SLOTS, 3)]
    small = pltpu.make_async_copy(numbers_hbm, out_numbers, in_sem.at[len(copies)])
    small.start()
    reads = [
        pltpu.make_async_copy(
            blocks_hbm.at[r, pl.ds(at.start, at.stop - at.start)],
            held.at[r, pl.ds(at.start, at.stop - at.start)], in_sem.at[c])
        for c, (r, at) in enumerate(copies)]
    writes = [
        pltpu.make_async_copy(
            held.at[r, pl.ds(at.start, at.stop - at.start)],
            out_hbm.at[r, pl.ds(at.start, at.stop - at.start)], out_sem.at[c])
        for c, (r, at) in enumerate(copies)]
    for c in reads:
        c.start()
    for before, after in zip(reads, writes):
        before.wait()
        after.start()
    for c in writes:
        c.wait()
    small.wait()


def hand_over(blocks, numbers):
    any_ = pl.BlockSpec(memory_space=pl.ANY)
    return pl.pallas_call(
        hand_over_kernel,
        out_shape=(
            jax.ShapeDtypeStruct(blocks.shape, blocks.dtype),
            jax.ShapeDtypeStruct(numbers.shape, numbers.dtype),
        ),
        in_specs=[any_, any_],
        out_specs=(any_, any_),
        scratch_shapes=[
            pltpu.VMEM((2, SLOTS, B, B), BF),
            pltpu.SemaphoreType.DMA((13,)), pltpu.SemaphoreType.DMA((12,)),
        ],
        compiler_params=pltpu.CompilerParams(vmem_limit_bytes=VMEM_LIMIT),
    )(blocks, numbers)


def per_device(fine_blocks, prolong_blocks, agg_start):
    return hand_over(*gather_all(fine_blocks, prolong_blocks, agg_start))


def solution(mesh):
    placed = (
        P(("wide", "narrow"), None, None, None),
        P(("wide", "narrow"), None, None, None),
        P(("wide", "narrow"), None),
    )
    return jax.shard_map(
        per_device,
        mesh=mesh,
        in_specs=placed,
        out_specs=(P(("wide", "narrow"), None, None, None), P(("wide", "narrow"))),
        check_vma=False,
    )
```

```python
import functools

import jax
import jax.numpy as jnp
from jax import lax
from jax.experimental import pallas as pl
from jax.experimental.pallas import tpu as pltpu
from jax.sharding import PartitionSpec as P

SLOTS = 17
ZDIM = 16
YDIM = 8
NDIM = 8
WDIM = 128
MID = 7
ROOT = 14
VMEM_LIMIT = 56 << 20
B = 192
W2 = 384
MESH = pl.DeviceIdType.MESH
BF = jnp.bfloat16
F32 = jnp.float32
COUNT_LANE = 4


def pack(x, y):
    lane = lax.broadcasted_iota(jnp.int32, (B, 128), 1)
    xh = jnp.concatenate([x[:, 128:].astype(F32), jnp.zeros((B, 64), F32)], axis=1)
    yh = jnp.concatenate([jnp.zeros((B, 64), F32), y[:, 128:].astype(F32)], axis=1)
    mid = jnp.where(lane < 64, xh, yh).astype(BF)
    return jnp.concatenate([x[:, :128], mid, y[:, :128]], axis=1)


def rows_first(pp):
    return jnp.concatenate([pp, jnp.zeros((64, W2), BF)], axis=0)


def rows_second(pp):
    return jnp.concatenate([jnp.zeros((64, W2), BF), pp[128:], pp[:128]], axis=0)


def mul(a, b):
    return jnp.dot(a, b, preferred_element_type=F32).astype(BF)


def exchange_kernel(
    a_hbm, p_hbm, start_ref,
    out_hbm, numbers,
    ints, prods, pt, acc, out, rank_tile, rank_smem, a_raw, p_raw, pp, pp_up, pp_dn, pp_s, pp_su,
    a_send, a_recv, one_recv, prod_recv,
    own_tile, g1, tile2, c_own, g2, t_own, o_in, g3, o_all, c_zero,
    local_sem, out_sem, ssem, rsem, gs, gr, ys, yr, cr, os, up_ready, low_ready, root_ready,
):
    w = lax.axis_index("wide")
    n = lax.axis_index("narrow")
    y = w // ZDIM
    z = w % ZDIM
    has_low = w > 0
    has_up = w < WDIM - 1
    low_w = jnp.maximum(w - 1, 0)
    up_w = jnp.minimum(w + 1, WDIM - 1)
    first = z == 0
    last = z == ZDIM - 1
    root = z == ROOT
    mid = z == MID
    below_mid = (z > 0) & (z < MID)
    root_at = (y * ZDIM + ROOT, n)
    mid_at = (y * ZDIM + MID, n)
    has_left = n > 0
    has_right = n < NDIM - 1
    left = jnp.maximum(n - 1, 0)
    right = jnp.minimum(n + 1, NDIM - 1)

    load_p = pltpu.make_async_copy(p_hbm, p_raw, local_sem.at[0])
    load_a = pltpu.make_async_copy(a_hbm, a_raw, local_sem.at[1])
    load_p.start()
    load_a.start()

    barrier = pltpu.get_barrier_semaphore()

    def greet(dev):
        pl.semaphore_signal(barrier, inc=1, device_id=dev, device_id_type=MESH)

    @pl.when(z < ZDIM - 1)
    def _():
        greet((up_w, n))

    for d in range(1, NDIM):
        greet((w, lax.rem(n + d, NDIM)))

    @pl.when(first & has_low)
    def _():
        greet((low_w, n))

    @pl.when(below_mid & (z < MID - 1))
    def _():
        greet(mid_at)

    @pl.when(z < ROOT - 1)
    def _():
        greet(root_at)

    @pl.when(root)
    def _():
        for d in range(1, YDIM):
            greet((lax.rem(y + d, YDIM) * ZDIM + ROOT, n))

    lane = lax.broadcasted_iota(jnp.int32, (8, 128), 1)
    sub = lax.broadcasted_iota(jnp.int32, (8, 128), 0)
    s00, s01, s10, s11 = (start_ref[i, j] for i in range(2) for j in range(2))
    count = (s00 == 2 * w).astype(jnp.int32) + (s10 == 2 * w + 1).astype(jnp.int32)
    tile = jnp.zeros((8, 128), jnp.int32)
    for at, value in enumerate((s00, s01, s10, s11, count)):
        tile = jnp.where(lane == at, value, tile)
    own_tile[...] = tile

    heard = (
        NDIM - 1
        + jnp.where(first, 0, 1)
        + jnp.where(mid, MID - 2, 0)
        + jnp.where(root, ROOT - 1 + YDIM - 1, 0)
        + jnp.where(last & has_up, 1, 0)
    )
    pl.semaphore_wait(barrier, heard)

    @pl.when(z > 0)
    def _():
        pl.semaphore_signal(up_ready, inc=1, device_id=(low_w, n), device_id_type=MESH)

    @pl.when(last & has_up)
    def _():
        pl.semaphore_signal(low_ready, inc=1, device_id=(up_w, n), device_id_type=MESH)

    def invite(at):
        pl.semaphore_signal(
            root_ready, inc=1, device_id=(y * ZDIM + at, n), device_id_type=MESH)

    @pl.when(mid)
    def _():
        for at in range(1, MID):
            invite(at)

    @pl.when(root)
    def _():
        for at in range(MID, ROOT):
            invite(at)

    load_p.wait()
    for r in range(2):
        pp[r] = pack(p_raw[r, 0], p_raw[r, 1])

    def remote(src, dst, at, dev):
        return pltpu.make_async_remote_copy(
            src_ref=src, dst_ref=dst, send_sem=ssem.at[at], recv_sem=rsem.at[at],
            device_id=dev, device_id_type=MESH)

    low, up = (low_w, n), (up_w, n)
    pp_low = remote(pp, pp_up, 0, low)
    pp_high = remote(pp.at[1], pp_dn, 1, up)
    pp_left = remote(pp, pp_s.at[1], 2, (w, left))
    pp_right = remote(pp, pp_s.at[0], 3, (w, right))
    rel_left = remote(pp_up, pp_su.at[1], 4, (w, left))
    rel_right = remote(pp_up, pp_su.at[0], 5, (w, right))
    a_low = [remote(a_send.at[q], a_recv.at[q], 6 + q, low) for q in range(4)]
    one_low = remote(a_raw.at[1, 1], one_recv, 10, low)
    prod_low = remote(prods.at[1, 2], prod_recv, 11, low)
    tile_low = remote(tile2, ints.at[pl.ds(16, 8)], 12, low)
    tile_high = remote(tile2, ints.at[pl.ds(0, 8)], 13, up)
    tile_rel = remote(ints.at[pl.ds(16, 8)], ints.at[pl.ds(24, 8)], 14, low)
    to_root = pltpu.make_async_remote_copy(
        src_ref=c_own, dst_ref=g2.at[z], send_sem=ssem.at[15], recv_sem=cr.at[z],
        device_id=(y * ZDIM + jnp.where(z < MID, MID, ROOT), n), device_id_type=MESH)
    from_root = remote(o_all.at[0], o_in, 16, root_at)

    zero_root = pltpu.make_async_remote_copy(
        src_ref=c_zero, dst_ref=g2.at[0], send_sem=os.at[0], recv_sem=cr.at[0],
        device_id=mid_at, device_id_type=MESH)

    def reply(at):
        return pltpu.make_async_remote_copy(
            src_ref=o_all.at[at], dst_ref=o_in, send_sem=os.at[at], recv_sem=rsem.at[16],
            device_id=(y * ZDIM + at, n), device_id_type=MESH)

    def arrived(at):
        return pltpu.make_async_remote_copy(
            src_ref=c_own, dst_ref=g2.at[at], send_sem=ssem.at[15], recv_sem=cr.at[at],
            device_id=root_at, device_id_type=MESH)

    others = [at for at in range(ZDIM) if at != ROOT]
    others = others[ROOT:] + others[:ROOT]
    half = pl.ds(0, MID + 1)
    mid_root = pltpu.make_async_remote_copy(
        src_ref=g2.at[half], dst_ref=g2.at[half], send_sem=os.at[0],
        recv_sem=rsem.at[17], device_id=root_at, device_id_type=MESH)

    gathers = []
    for d in range(1, NDIM):
        gathers.append(pltpu.make_async_remote_copy(
            src_ref=own_tile, dst_ref=g1.at[d], send_sem=gs.at[d], recv_sem=gr.at[d],
            device_id=(w, lax.rem(n + d, NDIM)), device_id_type=MESH))
    totals = []
    for d in range(1, YDIM):
        totals.append(pltpu.make_async_remote_copy(
            src_ref=t_own, dst_ref=g3.at[d], send_sem=ys.at[d], recv_sem=yr.at[d],
            device_id=(lax.rem(y + d, YDIM) * ZDIM + ROOT, n), device_id_type=MESH))

    for c in gathers:
        c.start()
    pl.when(has_low & ~first & ~last)(pp_low.start)
    pl.when(has_left)(pp_left.start)
    pl.when(has_right)(pp_right.start)

    load_a.wait()
    for q, ((i0, k0), (i1, k1)) in enumerate(
        (((0, 0), (0, 1)), ((0, 2), (1, 0)), ((0, 3), (0, 4)), ((1, 3), (1, 4)))):
        a_send[q] = pack(a_raw[i0, k0], a_raw[i1, k1])

    @pl.when(jnp.logical_not(has_up))
    def _():
        pp_up[...] = jnp.zeros_like(pp_up)
        a_recv[...] = jnp.zeros_like(a_recv)
        one_recv[...] = jnp.zeros_like(one_recv)
        prod_recv[...] = jnp.zeros_like(prod_recv)
        ints[16:32] = jnp.zeros((16, 128), jnp.int32)

    @pl.when(jnp.logical_not(has_low))
    def _():
        pp_dn[...] = jnp.zeros_like(pp_dn)
        ints[0:8] = jnp.zeros((8, 128), jnp.int32)

    for side, there in ((0, has_left), (1, has_right)):
        @pl.when(jnp.logical_not(there))
        def _():
            pp_s[side] = jnp.zeros((2, B, W2), BF)
            pp_su[side] = jnp.zeros((2, B, W2), BF)

    for c in gathers:
        c.wait_recv()
    g1[0] = own_tile[...]
    before = jnp.zeros((8, 128), jnp.int32)
    whole = own_tile[...]
    lines = jnp.where(sub == n, own_tile[...], 0)
    for d in range(1, NDIM):
        piece = g1[d]
        line = lax.rem(n + NDIM - d, NDIM)
        lines = jnp.where(sub == line, piece, lines)
        whole = whole + piece
        before = before + jnp.where(line < n, piece, 0)
    tile2[...] = lines
    ints[8:16] = lines
    c_own[...] = whole
    pl.when(z > ROOT)(to_root.start)
    pl.when(last)(pp_low.start)

    @pl.when(has_low & ~first)
    def _():
        tile_low.start()
        for q in range(4):
            a_low[q].start()
        one_low.start()

    @pl.when(~last)
    def _():
        pl.semaphore_wait(up_ready, 1)

    pl.when(has_up)(tile_high.start)
    pl.when(has_up)(pp_high.start)

    @pl.when(first & has_low)
    def _():
        pl.semaphore_wait(low_ready, 1)
        pp_low.start()
        tile_low.start()
        for q in range(4):
            a_low[q].start()
        one_low.start()

    def keep(i, k, value):
        prods[i, k] = value

    keep(0, 0, mul(a_raw[0, 0], pp[0]))
    keep(0, 2, mul(a_raw[0, 2], pp[1]))
    keep(1, 0, mul(a_raw[1, 0], pp[1]))
    keep(1, 1, mul(a_raw[1, 1], pp[0]))

    def transposed(at, block):
        t = block.astype(F32).T.astype(BF)
        pt[at, 0] = t[:B]
        pt[at, 1] = jnp.concatenate([t[256:], t[B:256]], axis=0)

    for r in range(2):
        transposed(r, pp[r])
    pl.when(has_left)(pp_right.wait_recv)
    for r in range(2):
        keep(r, 3, mul(a_raw[r, 3], pp_s[0, r]))
    pl.when(has_right)(pp_left.wait_recv)
    for r in range(2):
        keep(r, 4, mul(a_raw[r, 4], pp_s[1, r]))

    @pl.when(z == 1)
    def _():
        tile_high.wait_recv()
        c_zero[...] = jnp.broadcast_to(jnp.sum(ints[0:8], axis=0, keepdims=True), (8, 128))

    @pl.when((z > 0) & (z < ROOT))
    def _():
        pl.semaphore_wait(root_ready, 1)

    pl.when((z > 0) & (z < ROOT) & ~mid)(to_root.start)
    pl.when(z == 1)(zero_root.start)

    @pl.when(mid)
    def _():
        g2[MID] = c_own[...]
        for at in range(MID):
            arrived(at).wait_recv()
        mid_root.start()

    @pl.when(root)
    def _():
        g2[ROOT] = c_own[...]
        mid_root.wait_recv()
        for at in range(MID + 1, ZDIM):
            if at != ROOT:
                arrived(at).wait_recv()
        total = jnp.zeros((8, 128), jnp.int32)
        for at in range(ZDIM):
            o_all[at] = total
            total = total + g2[at]
        t_own[...] = total
        for c in totals:
            c.start()
        for c in totals:
            c.wait_recv()
        offset = jnp.zeros((8, 128), jnp.int32)
        for d in range(1, YDIM):
            offset = offset + jnp.where(lax.rem(y + YDIM - d, YDIM) < y, g3[d], 0)
        for at in range(ZDIM):
            o_all[at] = o_all[at] + offset
        o_in[...] = o_all[ROOT]
        for at in others:
            reply(at).start()

    pl.when(has_up)(pp_low.wait_recv)
    pl.when(has_left)(rel_left.start)
    pl.when(has_right)(rel_right.start)
    keep(1, 2, mul(a_raw[1, 2], pp_up[0]))
    pl.when(has_low)(prod_low.start)
    pl.when(has_up)(tile_low.wait_recv)
    pl.when(has_low)(tile_rel.start)
    for r in range(2):
        transposed(2 + r, pp_up[r])

    def halo(q, xp, x_at, y_at, yp):
        pl.when(has_up)(a_low[q].wait_recv)
        keep(*x_at, mul(a_recv[q, :, :256], rows_first(xp)))
        keep(*y_at, mul(a_recv[q, :, 128:], rows_second(yp)))

    halo(0, pp_up[0], (2, 0), (2, 1), pp[1])
    halo(1, pp_up[1], (2, 2), (3, 0), pp_up[1])
    pl.when(has_left)(rel_right.wait_recv)
    pl.when(has_right)(rel_left.wait_recv)
    halo(2, pp_su[0, 0], (2, 3), (2, 4), pp_su[1, 0])
    halo(3, pp_su[0, 1], (3, 3), (3, 4), pp_su[1, 1])
    pl.when(has_low)(pp_high.wait_recv)
    pl.when(has_low & (z != 1))(tile_high.wait_recv)
    keep(0, 1, mul(a_raw[0, 1], pp_dn[...]))
    pl.when(has_up)(one_low.wait_recv)
    keep(3, 1, mul(one_recv[...], pp_up[0]))
    pl.when(has_up)(prod_low.wait_recv)
    keep(3, 2, prod_recv[...])
    pl.when(has_up)(tile_rel.wait_recv)

    def start_of(line, rel, q):
        tile = ints[(rel + 2) // 2 * 8:(rel + 2) // 2 * 8 + 8]
        at = (rel % 2) * 2 + q
        chosen = jnp.where((sub == line) & (lane == at), tile, 0)
        return jnp.sum(jnp.sum(chosen, axis=1, keepdims=True), axis=0, keepdims=True)

    starts = {}
    for rel in range(-1, 5):
        for side in (-1, 0, 1) if 0 <= rel < 4 else (0,):
            for q in range(2):
                starts[rel, side, q] = start_of(n + side, rel, q)

    stores = []
    for r in range(2):
        acc[...] = jnp.zeros_like(acc)
        for ahead in range(3):
            i = r + ahead
            inside = 2 * w + i < 2 * WDIM
            left_sides = []
            for p in (1,) if ahead == 2 else (0, 1):
                mine = (starts[i, 0, p] == 2 * w + r) & inside
                chosen = jnp.where(mine, pt[i, p].astype(F32), 0.0).astype(BF)
                left_sides.append(chosen)
            for k in range(5):
                side = (0, 0, 0, -1, 1)[k]
                rel = i + (0, -1, 1, 0, 0)[k]
                x = 2 * w + rel
                there = (n + side >= 0) & (n + side < NDIM) & (x >= 0) & (x < 2 * WDIM)
                term = sum(
                    jnp.dot(c, prods[i, k], preferred_element_type=F32) for c in left_sides)

                def put(q, shift, r=r, k=k, rel=rel, there=there, term=term, side=side, x=x):
                    slot = (3, 3, 3, 9, 14)[k] + rel + shift - r
                    here = (starts[rel, side, q] == x + shift) & there
                    if q == 0:
                        acc[slot] += jnp.where(here, term[:, :B], 0.0)
                    else:
                        acc[slot, :, :128] += jnp.where(here, term[:, 256:], 0.0)
                        acc[slot, :, 128:] += jnp.where(here, term[:, B:256], 0.0)

                put(0, 0)
                put(0, -1)
                put(1, -1)
                put(1, -2)
                if rel == 0:
                    pl.when(w == 0)(functools.partial(put, 1, 0))
        out[r] = acc[...].astype(BF)
        stores.append(pltpu.make_async_copy(out.at[r], out_hbm.at[r], out_sem.at[r]))
        stores[r].start()

    pl.when(~root)(from_root.wait_recv)
    rank_tile[...] = o_in[...] + before
    ranks = pltpu.make_async_copy(rank_tile, rank_smem, local_sem.at[0])
    ranks.start()
    ranks.wait()
    rank = rank_smem[0, COUNT_LANE]
    begins = s00 == 2 * w
    numbers[0] = jnp.where(begins, rank, -1)
    numbers[1] = jnp.where(s10 == 2 * w + 1, rank + jnp.where(begins, 1, 0), -1)

    for c in gathers:
        c.wait_send()
    pl.when(has_low)(pp_low.wait_send)
    pl.when(has_up)(pp_high.wait_send)
    pl.when(has_left)(pp_left.wait_send)
    pl.when(has_right)(pp_right.wait_send)
    pl.when(has_left)(rel_left.wait_send)
    pl.when(has_right)(rel_right.wait_send)
    for c in a_low:
        pl.when(has_low)(c.wait_send)
    for c in (one_low, prod_low, tile_low, tile_rel):
        pl.when(has_low)(c.wait_send)
    pl.when(has_up)(tile_high.wait_send)
    pl.when(~root & ~first & ~mid)(to_root.wait_send)
    pl.when(mid)(mid_root.wait_send)
    pl.when(z == 1)(zero_root.wait_send)

    @pl.when(root)
    def _():
        for c in totals:
            c.wait_send()
        for at in others:
            reply(at).wait_send()

    for c in stores:
        c.wait()


def gather_all(fine_blocks, prolong_blocks, agg_start):
    smem = pl.BlockSpec(memory_space=pltpu.SMEM)
    any_ = pl.BlockSpec(memory_space=pl.ANY)
    i8 = pltpu.VMEM((8, 128), jnp.int32)

    def blocks(*lead):
        return pltpu.VMEM(lead + (B, W2), BF)

    def tiles(count):
        return pltpu.VMEM((count, 8, 128), jnp.int32)

    dma = pltpu.SemaphoreType.DMA
    regular = pltpu.SemaphoreType.REGULAR
    return pl.pallas_call(
        exchange_kernel,
        out_shape=(
            jax.ShapeDtypeStruct((2, SLOTS, B, B), BF),
            jax.ShapeDtypeStruct((2,), jnp.int32),
        ),
        in_specs=[any_, any_, smem],
        out_specs=(any_, smem),
        scratch_shapes=[
            pltpu.VMEM((32, 128), jnp.int32),
            blocks(4, 5), pltpu.VMEM((4, 2, B, B), BF),
            pltpu.VMEM((SLOTS, B, B), F32), pltpu.VMEM((2, SLOTS, B, B), BF),
            i8, pltpu.SMEM((8, 128), jnp.int32),
            pltpu.VMEM((2, 5, B, B), BF), pltpu.VMEM((2, 2, B, B), BF),
            blocks(2), blocks(2), blocks(), blocks(2, 2), blocks(2, 2),
            blocks(4), blocks(4), pltpu.VMEM((B, B), BF), blocks(),
            i8, tiles(NDIM), i8, i8, tiles(ZDIM), i8, i8, tiles(YDIM), tiles(ZDIM), i8,
            dma((2,)), dma((2,)), dma((17,)), dma((18,)), dma((NDIM,)), dma((NDIM,)),
            dma((YDIM,)), dma((YDIM,)), dma((ZDIM,)), dma((ZDIM,)),
            regular, regular, regular,
        ],
        compiler_params=pltpu.CompilerParams(
            collective_id=7, has_side_effects=True, vmem_limit_bytes=VMEM_LIMIT),
    )(fine_blocks, prolong_blocks, agg_start)


def hand_over_kernel(blocks_hbm, numbers_hbm, out_hbm, out_numbers, held, in_sem, out_sem):
    copies = [(r, slice(at, at + 1)) for r in range(2) for at in range(SLOTS)]
    small = pltpu.make_async_copy(numbers_hbm, out_numbers, in_sem.at[len(copies)])
    small.start()
    reads = [
        pltpu.make_async_copy(
            blocks_hbm.at[r, pl.ds(at.start, at.stop - at.start)],
            held.at[r, pl.ds(at.start, at.stop - at.start)], in_sem.at[c])
        for c, (r, at) in enumerate(copies)]
    writes = [
        pltpu.make_async_copy(
            held.at[r, pl.ds(at.start, at.stop - at.start)],
            out_hbm.at[r, pl.ds(at.start, at.stop - at.start)], out_sem.at[c])
        for c, (r, at) in enumerate(copies)]
    for c in reads:
        c.start()
    for before, after in zip(reads, writes):
        before.wait()
        after.start()
    for c in writes:
        c.wait()
    small.wait()


def hand_over(blocks, numbers):
    any_ = pl.BlockSpec(memory_space=pl.ANY)
    return pl.pallas_call(
        hand_over_kernel,
        out_shape=(
            jax.ShapeDtypeStruct(blocks.shape, blocks.dtype),
            jax.ShapeDtypeStruct(numbers.shape, numbers.dtype),
        ),
        in_specs=[any_, any_],
        out_specs=(any_, any_),
        scratch_shapes=[
            pltpu.VMEM((2, SLOTS, B, B), BF),
            pltpu.SemaphoreType.DMA((2 * SLOTS + 1,)), pltpu.SemaphoreType.DMA((2 * SLOTS,)),
        ],
        compiler_params=pltpu.CompilerParams(vmem_limit_bytes=VMEM_LIMIT),
    )(blocks, numbers)


def per_device(fine_blocks, prolong_blocks, agg_start):
    return hand_over(*gather_all(fine_blocks, prolong_blocks, agg_start))


def solution(mesh):
    placed = (
        P(("wide", "narrow"), None, None, None),
        P(("wide", "narrow"), None, None, None),
        P(("wide", "narrow"), None),
    )
    return jax.shard_map(
        per_device,
        mesh=mesh,
        in_specs=placed,
        out_specs=(P(("wide", "narrow"), None, None, None), P(("wide", "narrow"))),
        check_vma=False,
    )
```
